32 devices in a mesh: grp: 2 (over x), row: 8 (over z, y), col: 2 (over core).
Axes of the slice: x: 2, y: 2, z: 4, core: 2. Of those that a mesh axis runs over, the one named last changes fastest.
Arguments:
- score_panel: bfloat16 [2, 8, 2, 512, 128], P('grp', 'row', 'col'), parts along dimension 0, may hold values from -6 to 6
- blocks: bfloat16 [8, 2, 8, 512, 512], P('row', 'col'), may hold values from -0.09375 to 0.09375
- block_rows: int32 [8, 2, 8], P('row', 'col'), may hold values from 0 to 15, as said below
- block_cols: int32 [8, 2, 8], P('row', 'col'), may hold values from 0 to 15, as said below
- counts: int32 [8, 2], P('row', 'col'), may hold values from 1 to 8, as said below
- degrees: int32 [1, 8, 2, 512], replicated, may hold values from 1 to 4
Outputs:
- scores: bfloat16 [2, 8, 2, 512, 128], P('grp', 'row', 'col'), parts along dimension 0
The draws below stay inside these ranges and needn't reach their ends.
There are 2 independent parts, one for each index of `grp`. The reference program is written for one: setup_inputs(seed, part) draws one part's arguments, and reference() takes and returns one part's arrays. A program takes and returns all parts, laid end to end along the dimension named above; an argument that names none is the same for every part. Nothing has to cross between parts.
Inputs may be any that keep to these rules, and one draw needn't show every extreme that they name: `block_rows`: slot k of the cell with row index r and column index c names a block b with (b // 2) % 8 == r; below counts it is at most block_cols of that slot; pairs in a cell are distinct. `block_cols`: slot k of the cell with column index c names a block b with b % 2 == c; slots at or after counts name blocks of the same sets and carry no weight. `counts`: used slots come first in each cell; every cell uses at least one slot.
All inputs are finite; a program needn't handle non-finite values.
Results may differ from the reference program's by a relative error of at most 0.0041.
Values may be sent and summed in bfloat16 or wider, within the bound.
A program may use at most 64 MiB of HBM per device.

```python
import jax
import jax.numpy as jnp
from jax import lax

BLOCK_EDGE = 512
USER_COLS = 128
BLOCKS_DEV = 1
BLOCK_SLOTS = 8
ALL_BLOCKS = 16
N_ROW = 8
N_COL = 2


def block_pattern(key):
    stride = jnp.arange(BLOCKS_DEV)
    across = jnp.arange(N_COL)
    downward = jnp.arange(N_ROW)
    row_span = BLOCKS_DEV * N_COL
    col_span = BLOCKS_DEV * N_ROW
    row_global = (stride[None, :, None] * N_ROW + downward[:, None, None]) * N_COL + across[None, None, :]
    row_global = row_global.reshape(N_ROW, row_span)
    col_global = (stride[None, :, None] * N_ROW + downward[None, None, :]) * N_COL + across[:, None, None]
    col_global = col_global.reshape(N_COL, col_span)
    shape_full = (N_ROW, N_COL, row_span, col_span)
    row_choice = jnp.broadcast_to(row_global[:, None, :, None], shape_full).reshape(N_ROW, N_COL, row_span * col_span)
    col_choice = jnp.broadcast_to(col_global[None, :, None, :], shape_full).reshape(N_ROW, N_COL, row_span * col_span)
    valid = (row_choice <= col_choice).astype(jnp.int32)
    noise = jax.random.randint(key, row_choice.shape, 0, 1024, dtype=jnp.int32)
    ranking = valid * (1 << 24) + noise * 8192 + jnp.arange(row_span * col_span, dtype=jnp.int32)
    _, picked = lax.top_k(ranking, BLOCK_SLOTS)
    rows_out = jnp.take_along_axis(row_choice, picked, axis=-1).astype(jnp.int32)
    cols_out = jnp.take_along_axis(col_choice, picked, axis=-1).astype(jnp.int32)
    valid_count = jnp.sum(valid, axis=-1).astype(jnp.int32)
    count_key = jax.random.fold_in(key, 77)
    lowest = BLOCK_SLOTS // 2
    drawn = jax.random.randint(count_key, (N_ROW, N_COL), lowest, BLOCK_SLOTS + 1, dtype=jnp.int32)
    drawn = drawn.at[0, 0].set(BLOCK_SLOTS)
    drawn = drawn.at[N_ROW - 1, N_COL - 1].set(lowest)
    used = jnp.minimum(drawn, valid_count).astype(jnp.int32)
    return (rows_out, cols_out, used)


def draw_block_rows(key, part):
    return block_pattern(key)[0]


def draw_block_cols(key, part):
    return block_pattern(key)[1]


def draw_counts(key, part):
    return block_pattern(key)[2]


def with_ends(values, own_key, low, high):
    longest = values.shape.index(max(values.shape))
    spots = []
    for shift in (0, 1):
        where = [jax.random.randint(jax.random.fold_in(own_key, axis), (), 0, length) for axis, length in enumerate(values.shape)]
        where[longest] = (where[longest] + shift) % values.shape[longest]
        spots.append(tuple(where))
    return values.at[spots[0]].set(low).at[spots[1]].set(high)


def level_of(rng, shape, split, smallest, high):
    level, own = 1.0, jax.random.fold_in(rng, 6)
    for axis_at, shards_of in split:
        draws = jnp.exp(jax.random.uniform(jax.random.fold_in(own, axis_at), (shards_of,), jnp.float32, smallest / len(split), high / len(split)))
        level = level * jnp.repeat(draws, shape[axis_at] // shards_of).reshape([-1 if axis == axis_at else 1 for axis in range(len(shape))])
    return level


def scatter_about(key, shape, scale, most, shards=(), kind=jnp.bfloat16):
    factor_of = level_of(key, shape, shards, -0.22, 0.18) if shards else 1.0
    values = jax.random.normal(key, shape, jnp.float32) * scale * factor_of
    return jnp.minimum(jnp.maximum(values, -most), most).astype(kind)


def setup_inputs(seed: int = 0, part: int = 0) -> dict:
    keys = jax.random.split(jax.random.key(seed), 7)
    part_keys = jax.random.split(jax.random.fold_in(keys[6], part), 7)
    return {
        "score_panel": scatter_about(part_keys[0], (BLOCKS_DEV, N_ROW, N_COL, BLOCK_EDGE, USER_COLS), 1.0, 6.0, ((1, 8), (2, 2))),
        "blocks": scatter_about(keys[1], (N_ROW, N_COL, BLOCK_SLOTS, BLOCK_EDGE, BLOCK_EDGE), (BLOCK_SLOTS * BLOCK_EDGE) ** -0.5, 0.09375, ((0, 8), (1, 2))),
        "block_rows": draw_block_rows(jax.random.fold_in(keys[6], 71), part),
        "block_cols": draw_block_cols(jax.random.fold_in(keys[6], 71), part),
        "counts": draw_counts(jax.random.fold_in(keys[6], 71), part),
        "degrees": with_ends(jax.random.randint(keys[5], (BLOCKS_DEV, N_ROW, N_COL, BLOCK_EDGE), 1, 5), jax.random.fold_in(keys[5], 1), 1, 4).astype(jnp.int32),
    }


def apply_matrix(sent, tile_sets, row_ids, col_ids, slot_weight):

    def per_cell(running, element):
        tile_group, rows_here, cols_here, weight_here = element
        tile_float = tile_group.astype(jnp.float32)
        col_pick = sent[cols_here]
        row_pick = sent[rows_here]
        forward = jnp.einsum('kab,kbu->kau', tile_float, col_pick, precision=lax.Precision.HIGHEST)
        backward = jnp.einsum('kab,kau->kbu', tile_float, row_pick, precision=lax.Precision.HIGHEST)
        running = running.at[rows_here].add(weight_here[:, None, None] * forward)
        running = running.at[cols_here].add(weight_here[:, None, None] * backward)
        return (running, None)
    start = jnp.zeros(sent.shape, jnp.float32)
    total, _ = lax.scan(per_cell, start, (tile_sets, row_ids, col_ids, slot_weight))
    return total

def reference(score_panel, blocks, block_rows, block_cols, counts, degrees):
    cells = N_ROW * N_COL
    tile_sets = blocks.reshape(cells, BLOCK_SLOTS, BLOCK_EDGE, BLOCK_EDGE)
    row_ids = block_rows.reshape(cells, BLOCK_SLOTS).astype(jnp.int32)
    col_ids = block_cols.reshape(cells, BLOCK_SLOTS).astype(jnp.int32)
    in_use = jnp.arange(BLOCK_SLOTS)[None, :] < counts.reshape(cells, 1)
    slot_weight = jnp.where(in_use, jnp.where(row_ids == col_ids, 0.5, 1.0), 0.0).astype(jnp.float32)
    inv_root = lax.rsqrt(degrees.astype(jnp.float32)).reshape(ALL_BLOCKS, BLOCK_EDGE, 1)
    values = score_panel.reshape(ALL_BLOCKS, BLOCK_EDGE, USER_COLS).astype(jnp.float32)
    sent_first = (inv_root * values).astype(jnp.bfloat16)
    sent_first = lax.optimization_barrier(sent_first).astype(jnp.float32)
    first = inv_root * apply_matrix(sent_first, tile_sets, row_ids, col_ids, slot_weight)
    sent_second = (inv_root * first).astype(jnp.bfloat16)
    sent_second = lax.optimization_barrier(sent_second).astype(jnp.float32)
    second = apply_matrix(sent_second, tile_sets, row_ids, col_ids, slot_weight)
    scores = (first + inv_root * second).astype(jnp.bfloat16)
    return scores.reshape(score_panel.shape)
```

```python
import functools

import jax
import jax.numpy as jnp
from jax import lax
from jax.experimental import pallas as pl
from jax.experimental.pallas import tpu as pltpu
from jax.sharding import PartitionSpec as P

F32 = jnp.float32
BF16 = jnp.bfloat16


def kernel(
    row_count,
    slot_total,
    panel_ref,
    blocks_ref,
    rows_ref,
    cols_ref,
    counts_ref,
    degrees_ref,
    out_ref,
    tiles,
    gathered,
    mate_panel,
    y_out,
    y_in,
    z_out,
    z_in,
    own_terms,
    row_acc,
    mate_out,
    mate_in,
    first_keep,
    slot_of,
    weight_of,
    load_sem,
    gz_send,
    gz_recv,
    gy_send,
    gy_recv,
    gm_send,
    gm_recv,
    ry_send,
    ry_recv,
    rz_send,
    rz_recv,
    rm_send,
    rm_recv,
):
    r = lax.axis_index("row")
    c = lax.axis_index("col")
    z = r // 2
    y = r % 2
    levels = row_count // 2
    y_peer = r + 1 - 2 * y
    mate = 1 - c

    for k in range(slot_total):
        pltpu.make_async_copy(blocks_ref.at[0, 0, k], tiles.at[k], load_sem.at[k]).start()

    barrier = pltpu.get_barrier_semaphore()
    pl.semaphore_signal(barrier, inc=1, device_id={"col": mate})
    pl.semaphore_signal(barrier, inc=1, device_id={"row": y_peer})

    @pl.when(z > 0)
    def _():
        pl.semaphore_signal(barrier, inc=1, device_id={"row": r - 2})

    @pl.when(z < levels - 1)
    def _():
        pl.semaphore_signal(barrier, inc=1, device_id={"row": r + 2})

    pair = degrees_ref[0, r].astype(F32)
    inv = lax.rsqrt(jnp.where(c == 0, pair[0:1], pair[1:2]))
    panel = panel_ref[0, 0, 0].astype(F32).T
    gathered[0, r] = (inv * panel).astype(BF16)

    below = (z > 0).astype(jnp.int32)
    above = (z < levels - 1).astype(jnp.int32)
    pl.semaphore_wait(barrier, 2 + below + above)

    def remote(src, dst, send, recv, where):
        return pltpu.make_async_remote_copy(
            src_ref=src, dst_ref=dst, send_sem=send, recv_sem=recv, device_id=where
        )

    def gather_z(a, zp):
        ref = gathered.at[a, 2 * zp + y]
        return remote(ref, ref, gz_send.at[a, zp], gz_recv.at[a, zp], {"row": r - 2})

    def gather_y(a, zp):
        ref = gathered.at[a, 2 * zp + y]
        return remote(ref, ref, gy_send.at[a, zp], gy_recv.at[a, zp], {"row": y_peer})

    def arrive_y(a, zp):
        ref = gathered.at[a, 2 * zp + 1 - y]
        return remote(ref, ref, gy_send.at[a, zp], gy_recv.at[a, zp], {"row": y_peer})

    def gather_m(a):
        return remote(
            gathered.at[a, r], mate_panel.at[a], gm_send.at[a], gm_recv.at[a], {"col": mate}
        )

    def reduce_y(a, zp):
        return remote(
            y_out.at[a, zp], y_in.at[a, zp], ry_send.at[a, zp], ry_recv.at[a, zp], {"row": y_peer}
        )

    def reduce_z(a, zp):
        return remote(
            z_out.at[a, zp], z_in.at[a, zp], rz_send.at[a, zp], rz_recv.at[a, zp], {"row": r + 2}
        )

    def reduce_m(a):
        return remote(mate_out.at[a], mate_in.at[a], rm_send.at[a], rm_recv.at[a], {"col": mate})

    def start_gather(a):
        gather_m(a).start()

        @pl.when(z > 0)
        def _():
            gather_z(a, z).start()

        @pl.when(y == 1)
        def _():
            gather_y(a, z).start()

    start_gather(0)

    used = counts_ref[0, 0]

    def fill(rp, carry):
        for h in range(2):
            row_id = 2 * r + (c if h == 0 else mate)
            col_id = 2 * rp + c
            share = jnp.where(row_id == col_id, 0.5, 1.0).astype(F32)
            at = jnp.int32(0)
            weight = jnp.float32(0)
            for k in range(slot_total):
                hit = (rows_ref[0, 0, k] == row_id) & (cols_ref[0, 0, k] == col_id) & (k < used)
                at = jnp.where(hit, jnp.int32(k), at)
                weight = jnp.where(hit, share, weight)
            slot_of[h, rp] = at
            weight_of[h, rp] = weight
        return carry

    lax.fori_loop(r, row_count, fill, 0)

    for k in range(slot_total):
        pltpu.make_async_copy(blocks_ref.at[0, 0, k], tiles.at[k], load_sem.at[k]).wait()

    def transposed_term(a, rp):
        total = None
        for h in range(2):
            panel_h = gathered[a, r] if h == 0 else mate_panel[a]
            term = weight_of[h, rp] * jnp.dot(
                panel_h, tiles[slot_of[h, rp]], preferred_element_type=F32
            )
            total = term if total is None else total + term
        return total

    def add_forward(a, rp, fresh=False):
        for h in range(2):
            term = weight_of[h, rp] * lax.dot_general(
                gathered[a, rp],
                tiles[slot_of[h, rp]],
                (((1,), (1,)), ((), ())),
                preferred_element_type=F32,
            )
            if fresh:
                row_acc[h] = term
            else:
                row_acc[h] += term

    def apply(a):
        gather_m(a).wait_recv()

        def send_terms(s, carry):
            zp = levels - 1 - s
            y_out[a, zp] = transposed_term(a, 2 * zp + 1 - y).astype(BF16)
            reduce_y(a, zp).start()
            own_terms[zp] = transposed_term(a, 2 * zp + y)
            return carry

        lax.fori_loop(0, levels - 1 - z, send_terms, 0)

        @pl.when(y == 0)
        def _():
            y_out[a, z] = transposed_term(a, r + 1).astype(BF16)
            reduce_y(a, z).start()

        own_terms[z] = transposed_term(a, r)
        add_forward(a, r, fresh=True)

        def from_peer(zp):
            arrive_y(a, zp).wait_recv()
            add_forward(a, 2 * zp + 1 - y)

        def step(s, carry):
            zp = z + s
            gather_z(a, zp).wait_recv()

            @pl.when(z > 0)
            def _():
                gather_z(a, zp).start()

            gather_y(a, zp).start()
            zq = levels - s
            reduce_y(a, zq).wait_recv()
            summed = own_terms[zq] + y_in[a, zq].astype(F32)

            @pl.when(z > 0)
            def _():
                reduce_z(a, zq).wait_recv()
                z_out[a, zq] = (summed + z_in[a, zq].astype(F32)).astype(BF16)

            @pl.when(z == 0)
            def _():
                z_out[a, zq] = summed.astype(BF16)

            reduce_z(a, zq).start()
            add_forward(a, 2 * zp + y)

            @pl.when((s > 1) | (y == 0))
            def _():
                from_peer(zp - 1)

            return carry

        lax.fori_loop(1, levels - z, step, 0)

        @pl.when((z < levels - 1) | (y == 0))
        def _():
            from_peer(levels - 1)

        mate_out[a] = row_acc[1]
        reduce_m(a).start()
        row_acc[0] += own_terms[z]

        @pl.when(y == 1)
        def _():
            reduce_y(a, z).wait_recv()
            row_acc[0] += y_in[a, z].astype(F32)

        @pl.when(z > 0)
        def _():
            reduce_z(a, z).wait_recv()
            row_acc[0] += z_in[a, z].astype(F32)

        reduce_m(a).wait_recv()
        return inv * (row_acc[0] + mate_in[a])

    first = apply(0)
    first_keep[...] = first
    gathered[1, r] = (inv * first).astype(BF16)
    start_gather(1)
    second = apply(1)
    out_ref[0, 0, 0] = (first_keep[...] + second).T.astype(BF16)

    for a in range(2):
        gather_m(a).wait_send()
        reduce_m(a).wait_send()

        @pl.when(z > 0)
        def _():
            gather_z(a, z).wait_send()

        @pl.when(y == 1)
        def _():
            gather_y(a, z).wait_send()

        @pl.when(y == 0)
        def _():
            reduce_y(a, z).wait_send()

        def finish(zp, carry):
            @pl.when(z > 0)
            def _():
                gather_z(a, zp).wait_send()

            gather_y(a, zp).wait_send()
            reduce_y(a, zp).wait_send()
            reduce_z(a, zp).wait_send()
            return carry

        lax.fori_loop(z + 1, levels, finish, 0)


def shards(score_panel, blocks, block_rows, block_cols, counts, degrees):
    row_count = degrees.shape[1]
    levels = row_count // 2
    slot_total, edge = blocks.shape[2], blocks.shape[3]
    users = score_panel.shape[4]
    vmem = pl.BlockSpec(memory_space=pltpu.VMEM)
    smem = pl.BlockSpec(memory_space=pltpu.SMEM)
    dma = pltpu.SemaphoreType.DMA
    shape = (users, edge)
    return pl.pallas_call(
        functools.partial(kernel, row_count, slot_total),
        out_shape=jax.ShapeDtypeStruct(score_panel.shape, BF16),
        in_specs=[vmem, pl.BlockSpec(memory_space=pl.ANY), smem, smem, smem, vmem],
        out_specs=vmem,
        scratch_shapes=[
            pltpu.VMEM((slot_total, edge, edge), BF16),
            pltpu.VMEM((2, row_count) + shape, BF16),
            pltpu.VMEM((2,) + shape, BF16),
            pltpu.VMEM((2, levels) + shape, BF16),
            pltpu.VMEM((2, levels) + shape, BF16),
            pltpu.VMEM((2, levels) + shape, BF16),
            pltpu.VMEM((2, levels) + shape, BF16),
            pltpu.VMEM((levels,) + shape, F32),
            pltpu.VMEM((2,) + shape, F32),
            pltpu.VMEM((2,) + shape, F32),
            pltpu.VMEM((2,) + shape, F32),
            pltpu.VMEM(shape, F32),
            pltpu.SMEM((2, row_count), jnp.int32),
            pltpu.SMEM((2, row_count), F32),
            dma((slot_total,)),
            dma((2, levels)),
            dma((2, levels)),
            dma((2, levels)),
            dma((2, levels)),
            dma((2,)),
            dma((2,)),
            dma((2, levels)),
            dma((2, levels)),
            dma((2, levels)),
            dma((2, levels)),
            dma((2,)),
            dma((2,)),
        ],
        compiler_params=pltpu.CompilerParams(
            collective_id=0, has_side_effects=True, vmem_limit_bytes=56 * 1024 * 1024
        ),
    )(score_panel, blocks, block_rows, block_cols, counts, degrees)


def solution(mesh):
    in_specs = (
        P("grp", "row", "col", None, None),
        P("row", "col", None, None, None),
        P("row", "col", None),
        P("row", "col", None),
        P("row", "col"),
        P(),
    )
    out_specs = P("grp", "row", "col", None, None)
    return jax.shard_map(shards, mesh=mesh, in_specs=in_specs, out_specs=out_specs, check_vma=False)
```

```python
import functools

import jax
import jax.numpy as jnp
from jax import lax
from jax.experimental import pallas as pl
from jax.experimental.pallas import tpu as pltpu
from jax.sharding import PartitionSpec as P

F32 = jnp.float32
BF16 = jnp.bfloat16


def kernel(
    row_count,
    slot_total,
    panel_ref,
    blocks_ref,
    rows_ref,
    cols_ref,
    counts_ref,
    degrees_ref,
    out_ref,
    tiles,
    gathered,
    mate_panel,
    y_out,
    y_in,
    z_out,
    z_in,
    own_terms,
    row_acc,
    mate_out,
    mate_in,
    first_keep,
    slot_of,
    weight_of,
    load_sem,
    gz_send,
    gz_recv,
    gy_send,
    gy_recv,
    gm_send,
    gm_recv,
    ry_send,
    ry_recv,
    rz_send,
    rz_recv,
    rm_send,
    rm_recv,
):
    r = lax.axis_index("row")
    c = lax.axis_index("col")
    z = r // 2
    y = r % 2
    levels = row_count // 2
    y_peer = r + 1 - 2 * y
    mate = 1 - c

    for k in range(slot_total):
        pltpu.make_async_copy(blocks_ref.at[0, 0, k], tiles.at[k], load_sem.at[k]).start()

    barrier = pltpu.get_barrier_semaphore()
    pl.semaphore_signal(barrier, inc=1, device_id={"col": mate})
    pl.semaphore_signal(barrier, inc=1, device_id={"row": y_peer})

    def greet(s, carry):
        other = lax.rem(z + s, levels)
        pl.semaphore_signal(barrier, inc=1, device_id={"row": 2 * other + y})
        return carry

    lax.fori_loop(1, levels, greet, 0)

    pair = degrees_ref[0, r].astype(F32)
    inv = lax.rsqrt(jnp.where(c == 0, pair[0:1], pair[1:2]))
    panel = panel_ref[0, 0, 0].astype(F32).T
    gathered[0, r] = (inv * panel).astype(BF16)

    pl.semaphore_wait(barrier, levels + 1)

    def remote(src, dst, send, recv, where):
        return pltpu.make_async_remote_copy(
            src_ref=src, dst_ref=dst, send_sem=send, recv_sem=recv, device_id=where
        )

    def gather_z(a, zp):
        ref = gathered.at[a, r]
        return remote(ref, ref, gz_send.at[a, zp], gz_recv.at[a, z], {"row": 2 * zp + y})

    def arrive_z(a, zp):
        ref = gathered.at[a, 2 * zp + y]
        return remote(ref, ref, gz_send.at[a, zp], gz_recv.at[a, zp], {"row": 2 * zp + y})

    def gather_y(a, zp):
        ref = gathered.at[a, 2 * zp + y]
        return remote(ref, ref, gy_send.at[a, zp], gy_recv.at[a, zp], {"row": y_peer})

    def arrive_y(a, zp):
        ref = gathered.at[a, 2 * zp + 1 - y]
        return remote(ref, ref, gy_send.at[a, zp], gy_recv.at[a, zp], {"row": y_peer})

    def gather_m(a):
        return remote(
            gathered.at[a, r], mate_panel.at[a], gm_send.at[a], gm_recv.at[a], {"col": mate}
        )

    def reduce_y(a, zp):
        return remote(
            y_out.at[a, zp], y_in.at[a, zp], ry_send.at[a, zp], ry_recv.at[a, zp], {"row": y_peer}
        )

    def reduce_z(a, zp):
        return remote(
            z_out.at[a, zp],
            z_in.at[a, z],
            rz_send.at[a, zp],
            rz_recv.at[a, z],
            {"row": 2 * zp + y},
        )

    def arrive_reduce(a, zp):
        return remote(
            z_out.at[a, zp],
            z_in.at[a, zp],
            rz_send.at[a, zp],
            rz_recv.at[a, zp],
            {"row": 2 * zp + y},
        )

    def reduce_m(a):
        return remote(mate_out.at[a], mate_in.at[a], rm_send.at[a], rm_recv.at[a], {"col": mate})

    def start_gather(a):
        gather_m(a).start()

        @pl.when(y == 1)
        def _():
            gather_y(a, z).start()

        def down(zp, carry):
            gather_z(a, zp).start()
            return carry

        lax.fori_loop(0, z, down, 0)

    start_gather(0)

    used = counts_ref[0, 0]

    def fill(rp, carry):
        for h in range(2):
            row_id = 2 * r + (c if h == 0 else mate)
            col_id = 2 * rp + c
            share = jnp.where(row_id == col_id, 0.5, 1.0).astype(F32)
            at = jnp.int32(0)
            weight = jnp.float32(0)
            for k in range(slot_total):
                hit = (rows_ref[0, 0, k] == row_id) & (cols_ref[0, 0, k] == col_id) & (k < used)
                at = jnp.where(hit, jnp.int32(k), at)
                weight = jnp.where(hit, share, weight)
            slot_of[h, rp] = at
            weight_of[h, rp] = weight
        return carry

    lax.fori_loop(r, row_count, fill, 0)

    for k in range(slot_total):
        pltpu.make_async_copy(blocks_ref.at[0, 0, k], tiles.at[k], load_sem.at[k]).wait()

    def transposed_term(a, rp):
        total = None
        for h in range(2):
            panel_h = gathered[a, r] if h == 0 else mate_panel[a]
            term = weight_of[h, rp] * jnp.dot(
                panel_h, tiles[slot_of[h, rp]], preferred_element_type=F32
            )
            total = term if total is None else total + term
        return total

    def add_forward(a, rp, fresh=False):
        for h in range(2):
            term = weight_of[h, rp] * lax.dot_general(
                gathered[a, rp],
                tiles[slot_of[h, rp]],
                (((1,), (1,)), ((), ())),
                preferred_element_type=F32,
            )
            if fresh:
                row_acc[h] = term
            else:
                row_acc[h] += term

    def apply(a):
        gather_m(a).wait_recv()

        def send_terms(s, carry):
            zp = levels - 1 - s
            y_out[a, zp] = transposed_term(a, 2 * zp + 1 - y).astype(BF16)
            reduce_y(a, zp).start()
            own_terms[zp] = transposed_term(a, 2 * zp + y)
            return carry

        lax.fori_loop(0, levels - 1 - z, send_terms, 0)

        @pl.when(y == 0)
        def _():
            y_out[a, z] = transposed_term(a, r + 1).astype(BF16)
            reduce_y(a, z).start()

        own_terms[z] = transposed_term(a, r)
        add_forward(a, r, fresh=True)

        def from_peer(zp):
            arrive_y(a, zp).wait_recv()
            add_forward(a, 2 * zp + 1 - y)

        def step(s, carry):
            zp = z + s
            arrive_z(a, zp).wait_recv()
            gather_y(a, zp).start()
            zq = levels - s
            reduce_y(a, zq).wait_recv()
            z_out[a, zq] = (own_terms[zq] + y_in[a, zq].astype(F32)).astype(BF16)
            reduce_z(a, zq).start()
            add_forward(a, 2 * zp + y)

            @pl.when((s > 1) | (y == 0))
            def _():
                from_peer(zp - 1)

            return carry

        lax.fori_loop(1, levels - z, step, 0)

        @pl.when((z < levels - 1) | (y == 0))
        def _():
            from_peer(levels - 1)

        mate_out[a] = row_acc[1]
        reduce_m(a).start()
        row_acc[0] += own_terms[z]

        @pl.when(y == 1)
        def _():
            reduce_y(a, z).wait_recv()
            row_acc[0] += y_in[a, z].astype(F32)

        def from_below(zp, carry):
            arrive_reduce(a, zp).wait_recv()
            row_acc[0] += z_in[a, zp].astype(F32)
            return carry

        lax.fori_loop(0, z, from_below, 0)

        reduce_m(a).wait_recv()
        return inv * (row_acc[0] + mate_in[a])

    first = apply(0)
    first_keep[...] = first
    gathered[1, r] = (inv * first).astype(BF16)
    start_gather(1)
    second = apply(1)
    out_ref[0, 0, 0] = (first_keep[...] + second).T.astype(BF16)

    for a in range(2):
        gather_m(a).wait_send()
        reduce_m(a).wait_send()

        def sent_down(zp, carry):
            gather_z(a, zp).wait_send()
            return carry

        lax.fori_loop(0, z, sent_down, 0)

        @pl.when(y == 1)
        def _():
            gather_y(a, z).wait_send()

        @pl.when(y == 0)
        def _():
            reduce_y(a, z).wait_send()

        def finish(zp, carry):
            gather_y(a, zp).wait_send()
            reduce_y(a, zp).wait_send()
            reduce_z(a, zp).wait_send()
            return carry

        lax.fori_loop(z + 1, levels, finish, 0)


def shards(score_panel, blocks, block_rows, block_cols, counts, degrees):
    row_count = degrees.shape[1]
    levels = row_count // 2
    slot_total, edge = blocks.shape[2], blocks.shape[3]
    users = score_panel.shape[4]
    vmem = pl.BlockSpec(memory_space=pltpu.VMEM)
    smem = pl.BlockSpec(memory_space=pltpu.SMEM)
    dma = pltpu.SemaphoreType.DMA
    shape = (users, edge)
    return pl.pallas_call(
        functools.partial(kernel, row_count, slot_total),
        out_shape=jax.ShapeDtypeStruct(score_panel.shape, BF16),
        in_specs=[vmem, pl.BlockSpec(memory_space=pl.ANY), smem, smem, smem, vmem],
        out_specs=vmem,
        scratch_shapes=[
            pltpu.VMEM((slot_total, edge, edge), BF16),
            pltpu.VMEM((2, row_count) + shape, BF16),
            pltpu.VMEM((2,) + shape, BF16),
            pltpu.VMEM((2, levels) + shape, BF16),
            pltpu.VMEM((2, levels) + shape, BF16),
            pltpu.VMEM((2, levels) + shape, BF16),
            pltpu.VMEM((2, levels) + shape, BF16),
            pltpu.VMEM((levels,) + shape, F32),
            pltpu.VMEM((2,) + shape, F32),
            pltpu.VMEM((2,) + shape, F32),
            pltpu.VMEM((2,) + shape, F32),
            pltpu.VMEM(shape, F32),
            pltpu.SMEM((2, row_count), jnp.int32),
            pltpu.SMEM((2, row_count), F32),
            dma((slot_total,)),
            dma((2, levels)),
            dma((2, levels)),
            dma((2, levels)),
            dma((2, levels)),
            dma((2,)),
            dma((2,)),
            dma((2, levels)),
            dma((2, levels)),
            dma((2, levels)),
            dma((2, levels)),
            dma((2,)),
            dma((2,)),
        ],
        compiler_params=pltpu.CompilerParams(
            collective_id=0, has_side_effects=True, vmem_limit_bytes=56 * 1024 * 1024
        ),
    )(score_panel, blocks, block_rows, block_cols, counts, degrees)


def solution(mesh):
    in_specs = (
        P("grp", "row", "col", None, None),
        P("row", "col", None, None, None),
        P("row", "col", None),
        P("row", "col", None),
        P("row", "col"),
        P(),
    )
    out_specs = P("grp", "row", "col", None, None)
    return jax.shard_map(shards, mesh=mesh, in_specs=in_specs, out_specs=out_specs, check_vma=False)
```

```python
import functools

import jax
import jax.numpy as jnp
from jax import lax
from jax.experimental import pallas as pl
from jax.experimental.pallas import tpu as pltpu
from jax.sharding import PartitionSpec as P

F32 = jnp.float32
BF16 = jnp.bfloat16


def kernel(
    row_count,
    slot_total,
    panel_ref,
    blocks_ref,
    rows_ref,
    cols_ref,
    counts_ref,
    degrees_ref,
    out_ref,
    tiles,
    gathered,
    mate_panel,
    y_out,
    y_in,
    z_out,
    z_in,
    own_terms,
    row_acc,
    mate_out,
    mate_in,
    first_keep,
    far_in,
    far_got,
    slot_of,
    weight_of,
    load_sem,
    gz_send,
    gz_recv,
    gy_send,
    gy_recv,
    gm_send,
    gm_recv,
    ry_send,
    ry_recv,
    rz_send,
    rz_recv,
    rm_send,
    rm_recv,
    far_send,
    far_recv,
):
    r = lax.axis_index("row")
    c = lax.axis_index("col")
    z = r // 2
    y = r % 2
    levels = row_count // 2
    last = levels - 1
    y_peer = r + 1 - 2 * y
    mate = 1 - c

    for k in range(slot_total):
        pltpu.make_async_copy(blocks_ref.at[0, 0, k], tiles.at[k], load_sem.at[k]).start()

    barrier = pltpu.get_barrier_semaphore()
    pl.semaphore_signal(barrier, inc=1, device_id={"col": mate})
    pl.semaphore_signal(barrier, inc=1, device_id={"row": y_peer})

    def greet(s, carry):
        other = lax.rem(z + s, levels)
        pl.semaphore_signal(barrier, inc=1, device_id={"row": 2 * other + y})
        return carry

    lax.fori_loop(1, levels, greet, 0)

    pair = degrees_ref[0, r].astype(F32)
    inv = lax.rsqrt(jnp.where(c == 0, pair[0:1], pair[1:2]))
    panel = panel_ref[0, 0, 0].astype(F32).T
    gathered[0, r] = (inv * panel).astype(BF16)

    pl.semaphore_wait(barrier, levels + 1)

    def remote(src, dst, send, recv, where):
        return pltpu.make_async_remote_copy(
            src_ref=src, dst_ref=dst, send_sem=send, recv_sem=recv, device_id=where
        )

    def gather_z(a, zp):
        ref = gathered.at[a, r]
        return remote(ref, ref, gz_send.at[a, zp], gz_recv.at[a, z], {"row": 2 * zp + y})

    def arrive_z(a, zp):
        ref = gathered.at[a, 2 * zp + y]
        return remote(ref, ref, gz_send.at[a, zp], gz_recv.at[a, zp], {"row": 2 * zp + y})

    def gather_y(a, zp):
        ref = gathered.at[a, 2 * zp + y]
        return remote(ref, ref, gy_send.at[a, zp], gy_recv.at[a, zp], {"row": y_peer})

    def arrive_y(a, zp):
        ref = gathered.at[a, 2 * zp + 1 - y]
        return remote(ref, ref, gy_send.at[a, zp], gy_recv.at[a, zp], {"row": y_peer})

    def gather_m(a):
        return remote(
            gathered.at[a, r], mate_panel.at[a], gm_send.at[a], gm_recv.at[a], {"col": mate}
        )

    def reduce_y(a, zp):
        return remote(
            y_out.at[a, zp], y_in.at[a, zp], ry_send.at[a, zp], ry_recv.at[a, zp], {"row": y_peer}
        )

    def reduce_z(a, zp):
        return remote(
            z_out.at[a, zp],
            z_in.at[a, z],
            rz_send.at[a, zp],
            rz_recv.at[a, z],
            {"row": 2 * zp + y},
        )

    def arrive_reduce(a, zp):
        return remote(
            z_out.at[a, zp],
            z_in.at[a, zp],
            rz_send.at[a, zp],
            rz_recv.at[a, zp],
            {"row": 2 * zp + y},
        )

    def reduce_m(a):
        return remote(mate_out.at[a], mate_in.at[a], rm_send.at[a], rm_recv.at[a], {"col": mate})

    def far_panel(a, peer):
        ref = gathered.at[a, 2 * last + 1 - y]
        return remote(ref, ref, far_send.at[a, 0], far_recv.at[a, 0], {"row": 2 * peer + y})

    def far_term(a, peer):
        return remote(
            y_out.at[a, last],
            far_in.at[a],
            far_send.at[a, 1],
            far_recv.at[a, 1],
            {"row": 2 * peer + y},
        )

    def far_cross(a):
        return remote(
            far_in.at[a], far_got.at[a], far_send.at[a, 2], far_recv.at[a, 2], {"row": y_peer}
        )

    def start_gather(a):
        gather_m(a).start()

        @pl.when((y == 1) | (z == last))
        def _():
            gather_y(a, z).start()

        def down(zp, carry):
            gather_z(a, zp).start()
            return carry

        lax.fori_loop(0, z, down, 0)

    start_gather(0)

    used = counts_ref[0, 0]

    def fill(rp, carry):
        for h in range(2):
            row_id = 2 * r + (c if h == 0 else mate)
            col_id = 2 * rp + c
            share = jnp.where(row_id == col_id, 0.5, 1.0).astype(F32)
            at = jnp.int32(0)
            weight = jnp.float32(0)
            for k in range(slot_total):
                hit = (rows_ref[0, 0, k] == row_id) & (cols_ref[0, 0, k] == col_id) & (k < used)
                at = jnp.where(hit, jnp.int32(k), at)
                weight = jnp.where(hit, share, weight)
            slot_of[h, rp] = at
            weight_of[h, rp] = weight
        return carry

    lax.fori_loop(r, row_count, fill, 0)

    for k in range(slot_total):
        pltpu.make_async_copy(blocks_ref.at[0, 0, k], tiles.at[k], load_sem.at[k]).wait()

    def transposed_term(a, rp):
        total = None
        for h in range(2):
            panel_h = gathered[a, r] if h == 0 else mate_panel[a]
            term = weight_of[h, rp] * jnp.dot(
                panel_h, tiles[slot_of[h, rp]], preferred_element_type=F32
            )
            total = term if total is None else total + term
        return total

    def add_forward(a, rp, fresh=False):
        for h in range(2):
            term = weight_of[h, rp] * lax.dot_general(
                gathered[a, rp],
                tiles[slot_of[h, rp]],
                (((1,), (1,)), ((), ())),
                preferred_element_type=F32,
            )
            if fresh:
                row_acc[h] = term
            else:
                row_acc[h] += term

    def apply(a):
        @pl.when(z == last)
        def _():
            arrive_y(a, last).wait_recv()
            far_panel(a, 0).start()

        gather_m(a).wait_recv()

        @pl.when(z == 0)
        def _():
            y_out[a, last] = transposed_term(a, 2 * last + 1 - y).astype(BF16)
            far_term(a, last).start()
            z_out[a, last] = transposed_term(a, 2 * last + y).astype(BF16)
            reduce_z(a, last).start()

        skip = (z == 0).astype(jnp.int32)

        def send_terms(s, carry):
            zp = levels - 1 - s
            y_out[a, zp] = transposed_term(a, 2 * zp + 1 - y).astype(BF16)
            reduce_y(a, zp).start()
            own_terms[zp] = transposed_term(a, 2 * zp + y)
            return carry

        lax.fori_loop(skip, levels - 1 - z, send_terms, 0)

        @pl.when(y == 0)
        def _():
            y_out[a, z] = transposed_term(a, r + 1).astype(BF16)
            reduce_y(a, z).start()

        own_terms[z] = transposed_term(a, r)
        add_forward(a, r, fresh=True)

        @pl.when(z == last)
        def _():
            far_term(a, 0).wait_recv()
            far_cross(a).start()

        def from_peer(zp):
            arrive_y(a, zp).wait_recv()
            add_forward(a, 2 * zp + 1 - y)

        def step(s, carry):
            zp = z + s
            arrive_z(a, zp).wait_recv()

            @pl.when((z > 0) | (zp < last))
            def _():
                gather_y(a, zp).start()

            zq = levels - s - skip

            @pl.when(zq > z)
            def _():
                reduce_y(a, zq).wait_recv()
                z_out[a, zq] = (own_terms[zq] + y_in[a, zq].astype(F32)).astype(BF16)
                reduce_z(a, zq).start()

            add_forward(a, 2 * zp + y)

            @pl.when((s > 1) | (y == 0))
            def _():
                from_peer(zp - 1)

            return carry

        lax.fori_loop(1, levels - z, step, 0)

        @pl.when(((z > 0) & (z < last)) | ((z == last) & (y == 0)))
        def _():
            @pl.when(z < last)
            def _():
                arrive_y(a, last).wait_recv()

            add_forward(a, 2 * last + 1 - y)

        @pl.when(z == 0)
        def _():
            far_panel(a, last).wait_recv()
            add_forward(a, 2 * last + 1 - y)

        mate_out[a] = row_acc[1]
        reduce_m(a).start()
        row_acc[0] += own_terms[z]

        @pl.when(y == 1)
        def _():
            reduce_y(a, z).wait_recv()
            row_acc[0] += y_in[a, z].astype(F32)

        def from_below(zp, carry):
            arrive_reduce(a, zp).wait_recv()
            row_acc[0] += z_in[a, zp].astype(F32)
            return carry

        lax.fori_loop(0, z, from_below, 0)

        @pl.when(z == last)
        def _():
            far_cross(a).wait_recv()
            row_acc[0] += far_got[a].astype(F32)

        reduce_m(a).wait_recv()
        return inv * (row_acc[0] + mate_in[a])

    first = apply(0)
    first_keep[...] = first
    gathered[1, r] = (inv * first).astype(BF16)
    start_gather(1)
    second = apply(1)
    out_ref[0, 0, 0] = (first_keep[...] + second).T.astype(BF16)

    for a in range(2):
        gather_m(a).wait_send()
        reduce_m(a).wait_send()

        def sent_down(zp, carry):
            gather_z(a, zp).wait_send()
            return carry

        lax.fori_loop(0, z, sent_down, 0)

        @pl.when((y == 1) | (z == last))
        def _():
            gather_y(a, z).wait_send()

        @pl.when(z == 0)
        def _():
            far_term(a, last).wait_send()

        @pl.when(z == last)
        def _():
            far_panel(a, 0).wait_send()
            far_cross(a).wait_send()

        @pl.when(y == 0)
        def _():
            reduce_y(a, z).wait_send()

        def finish(zp, carry):
            @pl.when((z > 0) | (zp < last))
            def _():
                gather_y(a, zp).wait_send()
                reduce_y(a, zp).wait_send()

            reduce_z(a, zp).wait_send()
            return carry

        lax.fori_loop(z + 1, levels, finish, 0)


def shards(score_panel, blocks, block_rows, block_cols, counts, degrees):
    row_count = degrees.shape[1]
    levels = row_count // 2
    slot_total, edge = blocks.shape[2], blocks.shape[3]
    users = score_panel.shape[4]
    vmem = pl.BlockSpec(memory_space=pltpu.VMEM)
    smem = pl.BlockSpec(memory_space=pltpu.SMEM)
    dma = pltpu.SemaphoreType.DMA
    shape = (users, edge)
    return pl.pallas_call(
        functools.partial(kernel, row_count, slot_total),
        out_shape=jax.ShapeDtypeStruct(score_panel.shape, BF16),
        in_specs=[vmem, pl.BlockSpec(memory_space=pl.ANY), smem, smem, smem, vmem],
        out_specs=vmem,
        scratch_shapes=[
            pltpu.VMEM((slot_total, edge, edge), BF16),
            pltpu.VMEM((2, row_count) + shape, BF16),
            pltpu.VMEM((2,) + shape, BF16),
            pltpu.VMEM((2, levels) + shape, BF16),
            pltpu.VMEM((2, levels) + shape, BF16),
            pltpu.VMEM((2, levels) + shape, BF16),
            pltpu.VMEM((2, levels) + shape, BF16),
            pltpu.VMEM((levels,) + shape, F32),
            pltpu.VMEM((2,) + shape, F32),
            pltpu.VMEM((2,) + shape, F32),
            pltpu.VMEM((2,) + shape, F32),
            pltpu.VMEM(shape, F32),
            pltpu.VMEM((2,) + shape, BF16),
            pltpu.VMEM((2,) + shape, BF16),
            pltpu.SMEM((2, row_count), jnp.int32),
            pltpu.SMEM((2, row_count), F32),
            dma((slot_total,)),
            dma((2, levels)),
            dma((2, levels)),
            dma((2, levels)),
            dma((2, levels)),
            dma((2,)),
            dma((2,)),
            dma((2, levels)),
            dma((2, levels)),
            dma((2, levels)),
            dma((2, levels)),
            dma((2,)),
            dma((2,)),
            dma((2, 3)),
            dma((2, 3)),
        ],
        compiler_params=pltpu.CompilerParams(
            collective_id=0, has_side_effects=True, vmem_limit_bytes=56 * 1024 * 1024
        ),
    )(score_panel, blocks, block_rows, block_cols, counts, degrees)


def solution(mesh):
    in_specs = (
        P("grp", "row", "col", None, None),
        P("row", "col", None, None, None),
        P("row", "col", None),
        P("row", "col", None),
        P("row", "col"),
        P(),
    )
    out_specs = P("grp", "row", "col", None, None)
    return jax.shard_map(shards, mesh=mesh, in_specs=in_specs, out_specs=out_specs, check_vma=False)
```

```python
import functools

import jax
import jax.numpy as jnp
from jax import lax
from jax.experimental import pallas as pl
from jax.experimental.pallas import tpu as pltpu
from jax.sharding import PartitionSpec as P

F32 = jnp.float32
BF16 = jnp.bfloat16


def kernel(
    row_count,
    slot_total,
    panel_ref,
    blocks_ref,
    rows_ref,
    cols_ref,
    counts_ref,
    degrees_ref,
    out_ref,
    tiles,
    gathered,
    mate_panel,
    y_out,
    y_in,
    z_out,
    z_in,
    own_terms,
    row_acc,
    mate_out,
    mate_in,
    first_keep,
    far_in,
    far_got,
    slot_of,
    weight_of,
    load_sem,
    gz_send,
    gz_recv,
    gy_send,
    gy_recv,
    gm_send,
    gm_recv,
    ry_send,
    ry_recv,
    rz_send,
    rz_recv,
    rm_send,
    rm_recv,
    far_send,
    far_recv,
):
    r = lax.axis_index("row")
    c = lax.axis_index("col")
    z = r // 2
    y = r % 2
    levels = row_count // 2
    last = levels - 1
    y_peer = r + 1 - 2 * y
    mate = 1 - c

    for k in range(slot_total):
        pltpu.make_async_copy(blocks_ref.at[0, 0, k], tiles.at[k], load_sem.at[k]).start()

    barrier = pltpu.get_barrier_semaphore()
    pl.semaphore_signal(barrier, inc=1, device_id={"col": mate})
    pl.semaphore_signal(barrier, inc=1, device_id={"row": y_peer})

    def greet(s, carry):
        other = lax.rem(z + s, levels)
        pl.semaphore_signal(barrier, inc=1, device_id={"row": 2 * other + y})
        return carry

    lax.fori_loop(1, levels, greet, 0)

    pair = degrees_ref[0, r].astype(F32)
    inv = lax.rsqrt(jnp.where(c == 0, pair[0:1], pair[1:2]))
    panel = panel_ref[0, 0, 0].astype(F32).T
    gathered[0, r] = (inv * panel).astype(BF16)

    pl.semaphore_wait(barrier, levels + 1)

    def remote(src, dst, send, recv, where):
        return pltpu.make_async_remote_copy(
            src_ref=src, dst_ref=dst, send_sem=send, recv_sem=recv, device_id=where
        )

    def gather_z(a, zp):
        ref = gathered.at[a, r]
        return remote(ref, ref, gz_send.at[a, zp], gz_recv.at[a, z], {"row": 2 * zp + y})

    def arrive_z(a, zp):
        ref = gathered.at[a, 2 * zp + y]
        return remote(ref, ref, gz_send.at[a, zp], gz_recv.at[a, zp], {"row": 2 * zp + y})

    def gather_y(a, zp):
        ref = gathered.at[a, 2 * zp + y]
        return remote(ref, ref, gy_send.at[a, zp], gy_recv.at[a, zp], {"row": y_peer})

    def arrive_y(a, zp):
        ref = gathered.at[a, 2 * zp + 1 - y]
        return remote(ref, ref, gy_send.at[a, zp], gy_recv.at[a, zp], {"row": y_peer})

    def gather_m(a):
        return remote(
            gathered.at[a, r], mate_panel.at[a], gm_send.at[a], gm_recv.at[a], {"col": mate}
        )

    def reduce_y(a, zp):
        return remote(
            y_out.at[a, zp], y_in.at[a, zp], ry_send.at[a, zp], ry_recv.at[a, zp], {"row": y_peer}
        )

    def reduce_z(a, zp):
        return remote(
            z_out.at[a, zp],
            z_in.at[a, z],
            rz_send.at[a, zp],
            rz_recv.at[a, z],
            {"row": 2 * zp + y},
        )

    def arrive_reduce(a, zp):
        return remote(
            z_out.at[a, zp],
            z_in.at[a, zp],
            rz_send.at[a, zp],
            rz_recv.at[a, zp],
            {"row": 2 * zp + y},
        )

    def reduce_m(a):
        return remote(mate_out.at[a], mate_in.at[a], rm_send.at[a], rm_recv.at[a], {"col": mate})

    def far_panel(a, peer):
        ref = gathered.at[a, 2 * last + 1 - y]
        return remote(ref, ref, far_send.at[a, 0], far_recv.at[a, 0], {"row": 2 * peer + y})

    def far_term(a, peer):
        return remote(
            y_out.at[a, last],
            far_in.at[a],
            far_send.at[a, 1],
            far_recv.at[a, 1],
            {"row": 2 * peer + y},
        )

    def far_cross(a):
        return remote(
            far_in.at[a], far_got.at[a], far_send.at[a, 2], far_recv.at[a, 2], {"row": y_peer}
        )

    def start_gather(a):
        gather_m(a).start()

        @pl.when((y == 1) | (z == last))
        def _():
            gather_y(a, z).start()

        def down(zp, carry):
            gather_z(a, z - 1 - zp).start()
            return carry

        lax.fori_loop(0, z, down, 0)

    start_gather(0)

    used = counts_ref[0, 0]

    def fill(rp, carry):
        for h in range(2):
            row_id = 2 * r + (c if h == 0 else mate)
            col_id = 2 * rp + c
            share = jnp.where(row_id == col_id, 0.5, 1.0).astype(F32)
            at = jnp.int32(0)
            weight = jnp.float32(0)
            for k in range(slot_total):
                hit = (rows_ref[0, 0, k] == row_id) & (cols_ref[0, 0, k] == col_id) & (k < used)
                at = jnp.where(hit, jnp.int32(k), at)
                weight = jnp.where(hit, share, weight)
            slot_of[h, rp] = at
            weight_of[h, rp] = weight
        return carry

    lax.fori_loop(r, row_count, fill, 0)

    for k in range(slot_total):
        pltpu.make_async_copy(blocks_ref.at[0, 0, k], tiles.at[k], load_sem.at[k]).wait()

    def transposed_term(a, rp):
        total = None
        for h in range(2):
            panel_h = gathered[a, r] if h == 0 else mate_panel[a]
            term = weight_of[h, rp] * jnp.dot(
                panel_h, tiles[slot_of[h, rp]], preferred_element_type=F32
            )
            total = term if total is None else total + term
        return total

    def add_forward(a, rp, fresh=False):
        for h in range(2):
            term = weight_of[h, rp] * lax.dot_general(
                gathered[a, rp],
                tiles[slot_of[h, rp]],
                (((1,), (1,)), ((), ())),
                preferred_element_type=F32,
            )
            if fresh:
                row_acc[h] = term
            else:
                row_acc[h] += term

    def apply(a):
        @pl.when(z == last)
        def _():
            arrive_y(a, last).wait_recv()
            far_panel(a, 0).start()

        gather_m(a).wait_recv()

        @pl.when(z == 0)
        def _():
            y_out[a, last] = transposed_term(a, 2 * last + 1 - y).astype(BF16)
            far_term(a, last).start()
            z_out[a, last] = transposed_term(a, 2 * last + y).astype(BF16)
            reduce_z(a, last).start()

        skip = (z == 0).astype(jnp.int32)

        def send_terms(s, carry):
            zp = levels - 1 - s
            y_out[a, zp] = transposed_term(a, 2 * zp + 1 - y).astype(BF16)
            reduce_y(a, zp).start()
            own_terms[zp] = transposed_term(a, 2 * zp + y)
            return carry

        lax.fori_loop(skip, levels - 1 - z, send_terms, 0)

        @pl.when(y == 0)
        def _():
            y_out[a, z] = transposed_term(a, r + 1).astype(BF16)
            reduce_y(a, z).start()

        own_terms[z] = transposed_term(a, r)
        add_forward(a, r, fresh=True)

        @pl.when(z == last)
        def _():
            far_term(a, 0).wait_recv()
            far_cross(a).start()

        def from_peer(zp):
            arrive_y(a, zp).wait_recv()
            add_forward(a, 2 * zp + 1 - y)

        def step(s, carry):
            zp = z + s
            arrive_z(a, zp).wait_recv()

            @pl.when((z > 0) | (zp < last))
            def _():
                gather_y(a, zp).start()

            zq = levels - s - skip

            @pl.when(zq > z)
            def _():
                reduce_y(a, zq).wait_recv()
                z_out[a, zq] = (own_terms[zq] + y_in[a, zq].astype(F32)).astype(BF16)
                reduce_z(a, zq).start()

            add_forward(a, 2 * zp + y)

            @pl.when((s > 1) | (y == 0))
            def _():
                from_peer(zp - 1)

            return carry

        lax.fori_loop(1, levels - z, step, 0)

        @pl.when(((z > 0) & (z < last)) | ((z == last) & (y == 0)))
        def _():
            @pl.when(z < last)
            def _():
                arrive_y(a, last).wait_recv()

            add_forward(a, 2 * last + 1 - y)

        @pl.when(z == 0)
        def _():
            far_panel(a, last).wait_recv()
            add_forward(a, 2 * last + 1 - y)

        mate_out[a] = row_acc[1]
        reduce_m(a).start()
        row_acc[0] += own_terms[z]

        @pl.when(y == 1)
        def _():
            reduce_y(a, z).wait_recv()
            row_acc[0] += y_in[a, z].astype(F32)

        def from_below(zp, carry):
            arrive_reduce(a, zp).wait_recv()
            row_acc[0] += z_in[a, zp].astype(F32)
            return carry

        lax.fori_loop(0, z, from_below, 0)

        @pl.when(z == last)
        def _():
            far_cross(a).wait_recv()
            row_acc[0] += far_got[a].astype(F32)

        reduce_m(a).wait_recv()
        return inv * (row_acc[0] + mate_in[a])

    first = apply(0)
    first_keep[...] = first
    gathered[1, r] = (inv * first).astype(BF16)
    start_gather(1)
    second = apply(1)
    out_ref[0, 0, 0] = (first_keep[...] + second).T.astype(BF16)

    for a in range(2):
        gather_m(a).wait_send()
        reduce_m(a).wait_send()

        def sent_down(zp, carry):
            gather_z(a, zp).wait_send()
            return carry

        lax.fori_loop(0, z, sent_down, 0)

        @pl.when((y == 1) | (z == last))
        def _():
            gather_y(a, z).wait_send()

        @pl.when(z == 0)
        def _():
            far_term(a, last).wait_send()

        @pl.when(z == last)
        def _():
            far_panel(a, 0).wait_send()
            far_cross(a).wait_send()

        @pl.when(y == 0)
        def _():
            reduce_y(a, z).wait_send()

        def finish(zp, carry):
            @pl.when((z > 0) | (zp < last))
            def _():
                gather_y(a, zp).wait_send()
                reduce_y(a, zp).wait_send()

            reduce_z(a, zp).wait_send()
            return carry

        lax.fori_loop(z + 1, levels, finish, 0)


def shards(score_panel, blocks, block_rows, block_cols, counts, degrees):
    row_count = degrees.shape[1]
    levels = row_count // 2
    slot_total, edge = blocks.shape[2], blocks.shape[3]
    users = score_panel.shape[4]
    vmem = pl.BlockSpec(memory_space=pltpu.VMEM)
    smem = pl.BlockSpec(memory_space=pltpu.SMEM)
    dma = pltpu.SemaphoreType.DMA
    shape = (users, edge)
    return pl.pallas_call(
        functools.partial(kernel, row_count, slot_total),
        out_shape=jax.ShapeDtypeStruct(score_panel.shape, BF16),
        in_specs=[vmem, pl.BlockSpec(memory_space=pl.ANY), smem, smem, smem, vmem],
        out_specs=vmem,
        scratch_shapes=[
            pltpu.VMEM((slot_total, edge, edge), BF16),
            pltpu.VMEM((2, row_count) + shape, BF16),
            pltpu.VMEM((2,) + shape, BF16),
            pltpu.VMEM((2, levels) + shape, BF16),
            pltpu.VMEM((2, levels) + shape, BF16),
            pltpu.VMEM((2, levels) + shape, BF16),
            pltpu.VMEM((2, levels) + shape, BF16),
            pltpu.VMEM((levels,) + shape, F32),
            pltpu.VMEM((2,) + shape, F32),
            pltpu.VMEM((2,) + shape, F32),
            pltpu.VMEM((2,) + shape, F32),
            pltpu.VMEM(shape, F32),
            pltpu.VMEM((2,) + shape, BF16),
            pltpu.VMEM((2,) + shape, BF16),
            pltpu.SMEM((2, row_count), jnp.int32),
            pltpu.SMEM((2, row_count), F32),
            dma((slot_total,)),
            dma((2, levels)),
            dma((2, levels)),
            dma((2, levels)),
            dma((2, levels)),
            dma((2,)),
            dma((2,)),
            dma((2, levels)),
            dma((2, levels)),
            dma((2, levels)),
            dma((2, levels)),
            dma((2,)),
            dma((2,)),
            dma((2, 3)),
            dma((2, 3)),
        ],
        compiler_params=pltpu.CompilerParams(
            collective_id=0, has_side_effects=True, vmem_limit_bytes=56 * 1024 * 1024
        ),
    )(score_panel, blocks, block_rows, block_cols, counts, degrees)


def solution(mesh):
    in_specs = (
        P("grp", "row", "col", None, None),
        P("row", "col", None, None, None),
        P("row", "col", None),
        P("row", "col", None),
        P("row", "col"),
        P(),
    )
    out_specs = P("grp", "row", "col", None, None)
    return jax.shard_map(shards, mesh=mesh, in_specs=in_specs, out_specs=out_specs, check_vma=False)
```

```python
import functools

import jax
import jax.numpy as jnp
from jax import lax
from jax.experimental import pallas as pl
from jax.experimental.pallas import tpu as pltpu
from jax.sharding import PartitionSpec as P

F32 = jnp.float32
BF16 = jnp.bfloat16


def kernel(
    row_count,
    slot_total,
    panel_ref,
    blocks_ref,
    rows_ref,
    cols_ref,
    counts_ref,
    degrees_ref,
    out_ref,
    tiles,
    gathered,
    mate_panel,
    y_out,
    y_in,
    z_out,
    z_in,
    own_terms,
    row_acc,
    mate_out,
    mate_in,
    first_keep,
    far_in,
    far_got,
    slot_of,
    weight_of,
    load_sem,
    gz_send,
    gz_recv,
    gy_send,
    gy_recv,
    gm_send,
    gm_recv,
    ry_send,
    ry_recv,
    rz_send,
    rz_recv,
    rm_send,
    rm_recv,
    far_send,
    far_recv,
    hub_send,
):
    r = lax.axis_index("row")
    c = lax.axis_index("col")
    z = r // 2
    y = r % 2
    levels = row_count // 2
    last = levels - 1
    at_last = (z == last).astype(jnp.int32)
    y_peer = r + 1 - 2 * y
    mate = 1 - c

    for k in range(slot_total):
        pltpu.make_async_copy(blocks_ref.at[0, 0, k], tiles.at[k], load_sem.at[k]).start()

    barrier = pltpu.get_barrier_semaphore()
    pl.semaphore_signal(barrier, inc=1, device_id={"col": mate})
    pl.semaphore_signal(barrier, inc=1, device_id={"row": y_peer})

    def greet(s, carry):
        other = lax.rem(z + s, levels)
        pl.semaphore_signal(barrier, inc=1, device_id={"row": 2 * other + y})
        return carry

    lax.fori_loop(1, levels, greet, 0)

    pair = degrees_ref[0, r].astype(F32)
    inv = lax.rsqrt(jnp.where(c == 0, pair[0:1], pair[1:2]))
    panel = panel_ref[0, 0, 0].astype(F32).T
    gathered[0, r] = (inv * panel).astype(BF16)

    pl.semaphore_wait(barrier, levels + 1)

    def remote(src, dst, send, recv, where):
        return pltpu.make_async_remote_copy(
            src_ref=src, dst_ref=dst, send_sem=send, recv_sem=recv, device_id=where
        )

    def gather_z(a, zp):
        ref = gathered.at[a, r]
        return remote(ref, ref, gz_send.at[a, zp], gz_recv.at[a, z], {"row": 2 * zp + y})

    def arrive_z(a, zp):
        ref = gathered.at[a, 2 * zp + y]
        return remote(ref, ref, gz_send.at[a, zp], gz_recv.at[a, zp], {"row": 2 * zp + y})

    def gather_y(a, zp):
        ref = gathered.at[a, 2 * zp + y]
        return remote(ref, ref, gy_send.at[a, zp], gy_recv.at[a, zp], {"row": y_peer})

    def arrive_y(a, zp):
        ref = gathered.at[a, 2 * zp + 1 - y]
        return remote(ref, ref, gy_send.at[a, zp], gy_recv.at[a, zp], {"row": y_peer})

    def gather_m(a):
        return remote(
            gathered.at[a, r], mate_panel.at[a], gm_send.at[a], gm_recv.at[a], {"col": mate}
        )

    def reduce_y(a, zp):
        return remote(
            y_out.at[a, zp], y_in.at[a, zp], ry_send.at[a, zp], ry_recv.at[a, zp], {"row": y_peer}
        )

    def reduce_z(a, zp):
        return remote(
            z_out.at[a, zp],
            z_in.at[a, z],
            rz_send.at[a, zp],
            rz_recv.at[a, z],
            {"row": 2 * zp + y},
        )

    def arrive_reduce(a, zp):
        return remote(
            z_out.at[a, zp],
            z_in.at[a, zp],
            rz_send.at[a, zp],
            rz_recv.at[a, zp],
            {"row": 2 * zp + y},
        )

    def reduce_m(a):
        return remote(mate_out.at[a], mate_in.at[a], rm_send.at[a], rm_recv.at[a], {"col": mate})

    def far_panel(a, peer):
        ref = gathered.at[a, 2 * last + 1 - y]
        return remote(ref, ref, far_send.at[a, 0], far_recv.at[a, 0], {"row": 2 * peer + y})

    def hub_panel(a, which):
        ref = gathered.at[a, 2 * last + (y if which == 0 else 1 - y)]
        recv = gz_recv.at[a, last] if which == 0 else far_recv.at[a, 0]
        return remote(ref, ref, hub_send.at[a, which], recv, {"row": y})

    def far_term(a, peer):
        return remote(
            y_out.at[a, last],
            far_in.at[a],
            far_send.at[a, 1],
            far_recv.at[a, 1],
            {"row": 2 * peer + y},
        )

    def far_cross(a):
        return remote(
            far_in.at[a], far_got.at[a], far_send.at[a, 2], far_recv.at[a, 2], {"row": y_peer}
        )

    def start_gather(a):
        gather_m(a).start()

        @pl.when((y == 1) | (z == last))
        def _():
            gather_y(a, z).start()

        def down(zp, carry):
            gather_z(a, z - 1 - zp).start()
            return carry

        lax.fori_loop(0, z - at_last, down, 0)

    start_gather(0)

    used = counts_ref[0, 0]

    def fill(rp, carry):
        for h in range(2):
            row_id = 2 * r + (c if h == 0 else mate)
            col_id = 2 * rp + c
            share = jnp.where(row_id == col_id, 0.5, 1.0).astype(F32)
            at = jnp.int32(0)
            weight = jnp.float32(0)
            for k in range(slot_total):
                hit = (rows_ref[0, 0, k] == row_id) & (cols_ref[0, 0, k] == col_id) & (k < used)
                at = jnp.where(hit, jnp.int32(k), at)
                weight = jnp.where(hit, share, weight)
            slot_of[h, rp] = at
            weight_of[h, rp] = weight
        return carry

    lax.fori_loop(r, row_count, fill, 0)

    for k in range(slot_total):
        pltpu.make_async_copy(blocks_ref.at[0, 0, k], tiles.at[k], load_sem.at[k]).wait()

    def transposed_term(a, rp):
        total = None
        for h in range(2):
            panel_h = gathered[a, r] if h == 0 else mate_panel[a]
            term = weight_of[h, rp] * jnp.dot(
                panel_h, tiles[slot_of[h, rp]], preferred_element_type=F32
            )
            total = term if total is None else total + term
        return total

    def add_forward(a, rp, fresh=False):
        for h in range(2):
            term = weight_of[h, rp] * lax.dot_general(
                gathered[a, rp],
                tiles[slot_of[h, rp]],
                (((1,), (1,)), ((), ())),
                preferred_element_type=F32,
            )
            if fresh:
                row_acc[h] = term
            else:
                row_acc[h] += term

    def apply(a):
        @pl.when(z == last)
        def _():
            arrive_y(a, last).wait_recv()
            far_panel(a, 1).start()

        gather_m(a).wait_recv()

        @pl.when(z == 0)
        def _():
            y_out[a, last] = transposed_term(a, 2 * last + 1 - y).astype(BF16)
            far_term(a, last).start()
            z_out[a, last] = transposed_term(a, 2 * last + y).astype(BF16)
            reduce_z(a, last).start()

        skip = (z == 0).astype(jnp.int32)

        def send_terms(s, carry):
            zp = levels - 1 - s
            y_out[a, zp] = transposed_term(a, 2 * zp + 1 - y).astype(BF16)
            reduce_y(a, zp).start()
            own_terms[zp] = transposed_term(a, 2 * zp + y)
            return carry

        lax.fori_loop(skip, levels - 1 - z, send_terms, 0)

        @pl.when(y == 0)
        def _():
            y_out[a, z] = transposed_term(a, r + 1).astype(BF16)
            reduce_y(a, z).start()

        own_terms[z] = transposed_term(a, r)
        add_forward(a, r, fresh=True)

        @pl.when(z == last)
        def _():
            far_term(a, 0).wait_recv()
            far_cross(a).start()

        def from_peer(zp):
            arrive_y(a, zp).wait_recv()
            add_forward(a, 2 * zp + 1 - y)

        def step(s, carry):
            zp = z + s
            arrive_z(a, zp).wait_recv()

            @pl.when((z > 1) | (zp < last))
            def _():
                gather_y(a, zp).start()

            @pl.when((z == 1) & (zp == last))
            def _():
                hub_panel(a, 0).start()
                far_panel(a, last).wait_recv()
                hub_panel(a, 1).start()

            zq = levels - s - skip

            @pl.when(zq > z)
            def _():
                reduce_y(a, zq).wait_recv()
                z_out[a, zq] = (own_terms[zq] + y_in[a, zq].astype(F32)).astype(BF16)
                reduce_z(a, zq).start()

            add_forward(a, 2 * zp + y)

            @pl.when((s > 1) | (y == 0))
            def _():
                from_peer(zp - 1)

            return carry

        lax.fori_loop(1, levels - z, step, 0)

        @pl.when(((z > 0) & (z < last)) | ((z == last) & (y == 0)))
        def _():
            @pl.when((z > 1) & (z < last))
            def _():
                arrive_y(a, last).wait_recv()

            add_forward(a, 2 * last + 1 - y)

        @pl.when(z == 0)
        def _():
            far_panel(a, last).wait_recv()
            add_forward(a, 2 * last + 1 - y)

        mate_out[a] = row_acc[1]
        reduce_m(a).start()
        row_acc[0] += own_terms[z]

        @pl.when(y == 1)
        def _():
            reduce_y(a, z).wait_recv()
            row_acc[0] += y_in[a, z].astype(F32)

        def from_below(zp, carry):
            arrive_reduce(a, zp).wait_recv()
            row_acc[0] += z_in[a, zp].astype(F32)
            return carry

        lax.fori_loop(0, z, from_below, 0)

        @pl.when(z == last)
        def _():
            far_cross(a).wait_recv()
            row_acc[0] += far_got[a].astype(F32)

        reduce_m(a).wait_recv()
        return inv * (row_acc[0] + mate_in[a])

    first = apply(0)
    first_keep[...] = first
    gathered[1, r] = (inv * first).astype(BF16)
    start_gather(1)
    second = apply(1)
    out_ref[0, 0, 0] = (first_keep[...] + second).T.astype(BF16)

    for a in range(2):
        gather_m(a).wait_send()
        reduce_m(a).wait_send()

        def sent_down(zp, carry):
            gather_z(a, zp).wait_send()
            return carry

        lax.fori_loop(at_last, z, sent_down, 0)

        @pl.when((y == 1) | (z == last))
        def _():
            gather_y(a, z).wait_send()

        @pl.when(z == 0)
        def _():
            far_term(a, last).wait_send()

        @pl.when(z == 1)
        def _():
            hub_panel(a, 0).wait_send()
            hub_panel(a, 1).wait_send()

        @pl.when(z == last)
        def _():
            far_panel(a, 1).wait_send()
            far_cross(a).wait_send()

        @pl.when(y == 0)
        def _():
            reduce_y(a, z).wait_send()

        def finish(zp, carry):
            @pl.when((z > 1) | (zp < last))
            def _():
                gather_y(a, zp).wait_send()

            @pl.when((z > 0) | (zp < last))
            def _():
                reduce_y(a, zp).wait_send()

            reduce_z(a, zp).wait_send()
            return carry

        lax.fori_loop(z + 1, levels, finish, 0)


def shards(score_panel, blocks, block_rows, block_cols, counts, degrees):
    row_count = degrees.shape[1]
    levels = row_count // 2
    slot_total, edge = blocks.shape[2], blocks.shape[3]
    users = score_panel.shape[4]
    vmem = pl.BlockSpec(memory_space=pltpu.VMEM)
    smem = pl.BlockSpec(memory_space=pltpu.SMEM)
    dma = pltpu.SemaphoreType.DMA
    shape = (users, edge)
    return pl.pallas_call(
        functools.partial(kernel, row_count, slot_total),
        out_shape=jax.ShapeDtypeStruct(score_panel.shape, BF16),
        in_specs=[vmem, pl.BlockSpec(memory_space=pl.ANY), smem, smem, smem, vmem],
        out_specs=vmem,
        scratch_shapes=[
            pltpu.VMEM((slot_total, edge, edge), BF16),
            pltpu.VMEM((2, row_count) + shape, BF16),
            pltpu.VMEM((2,) + shape, BF16),
            pltpu.VMEM((2, levels) + shape, BF16),
            pltpu.VMEM((2, levels) + shape, BF16),
            pltpu.VMEM((2, levels) + shape, BF16),
            pltpu.VMEM((2, levels) + shape, BF16),
            pltpu.VMEM((levels,) + shape, F32),
            pltpu.VMEM((2,) + shape, F32),
            pltpu.VMEM((2,) + shape, F32),
            pltpu.VMEM((2,) + shape, F32),
            pltpu.VMEM(shape, F32),
            pltpu.VMEM((2,) + shape, BF16),
            pltpu.VMEM((2,) + shape, BF16),
            pltpu.SMEM((2, row_count), jnp.int32),
            pltpu.SMEM((2, row_count), F32),
            dma((slot_total,)),
            dma((2, levels)),
            dma((2, levels)),
            dma((2, levels)),
            dma((2, levels)),
            dma((2,)),
            dma((2,)),
            dma((2, levels)),
            dma((2, levels)),
            dma((2, levels)),
            dma((2, levels)),
            dma((2,)),
            dma((2,)),
            dma((2, 3)),
            dma((2, 3)),
            dma((2, 2)),
        ],
        compiler_params=pltpu.CompilerParams(
            collective_id=0, has_side_effects=True, vmem_limit_bytes=56 * 1024 * 1024
        ),
    )(score_panel, blocks, block_rows, block_cols, counts, degrees)


def solution(mesh):
    in_specs = (
        P("grp", "row", "col", None, None),
        P("row", "col", None, None, None),
        P("row", "col", None),
        P("row", "col", None),
        P("row", "col"),
        P(),
    )
    out_specs = P("grp", "row", "col", None, None)
    return jax.shard_map(shards, mesh=mesh, in_specs=in_specs, out_specs=out_specs, check_vma=False)
```
